128 devices in a mesh: rows: 16 (over x_hi, y, core), feat: 8 (over z, x_lo).
Axes of the slice: x: 4 (x_hi: 2, x_lo: 2; x = x_hi * 2 + x_lo), y: 4, z: 4, core: 2. Of those that a mesh axis runs over, the one named last changes fastest.
Arguments:
- activations: bfloat16 [512, 96, 8192], P('rows', None, 'feat'), may hold values from -6 to 6
- out_grads: bfloat16 [512, 96, 8192], P('rows', None, 'feat'), may hold values from -6 to 6
- proj_in: bfloat16 [8192, 128], P('feat'), may hold values from -0.0625 to 0.0625
- proj_out: bfloat16 [8192, 128], P('feat'), may hold values from -0.0625 to 0.0625
- lengths: int32 [512], P('rows'), may hold values from 12 to 96
- hess_tiles: bfloat16 [16, 1024, 1024], P('feat'), may hold values from -3 to 3
- train_grads: bfloat16 [32768, 16384], P('rows', 'feat'), may hold values from -6 to 6
Outputs:
- scores: float32 [512, 32768], P('feat', 'rows')
The draws below stay inside these ranges and needn't reach their ends.
All inputs are finite; a program needn't handle non-finite values.
Results may differ from the reference program's by a relative error of at most 0.0057.
Values may be sent and summed in bfloat16 or wider, within the bound.
A program may use at most 128 MiB of HBM per device.

```python
import jax
import jax.numpy as jnp
from jax import lax

D = 8192
R = 128
BLK = 1024
SEQ = 96
QUERIES = 512
NTRAIN = 32768
FEATS = 16384
NBLK = 16


def draw_lengths(key, part):
    values = jax.random.randint(key, (QUERIES,), SEQ // 8, SEQ + 1)
    return values.at[0].set(SEQ).at[1].set(SEQ // 8).astype(jnp.int32)


def draw_hess_tiles(key, part):
    key_diag, key_off = jax.random.split(jax.random.fold_in(key, 11))
    diag = jax.random.uniform(key_diag, (NBLK, BLK), minval=1.0, maxval=2.0)
    off = jax.random.normal(key_off, (NBLK, BLK, BLK)) * (0.7 / jnp.sqrt(jnp.float32(BLK)))
    tiles = off + diag[:, :, None] * jnp.eye(BLK, dtype=jnp.float32)[None, :, :]
    return jnp.clip(tiles, -3.0, 3.0).astype(jnp.bfloat16)


def steps_of(own_key, shape, cuts, smallest, top_value):
    loudness = 1.0
    for dim, blocks in cuts:
        steps = jax.random.uniform(jax.random.fold_in(jax.random.fold_in(own_key, 6), dim), (blocks,), jnp.float32, smallest / len(cuts), top_value / len(cuts))
        loudness = loudness * jnp.repeat(jnp.exp(steps), shape[dim] // blocks).reshape((-1,) + (1,) * (len(shape) - 1 - dim))
    return loudness


def scatter_about(key, extent, scale, limit, cuts=(), kind=jnp.bfloat16):
    result = scale * jax.random.normal(key, extent, jnp.float32)
    if cuts:
        result = result * steps_of(key, extent, cuts, -0.22, 0.18)
    return jnp.clip(result, -limit, limit).astype(kind)


def setup_inputs(seed: int = 0) -> dict:
    splits = jax.random.split(jax.random.key(seed), 8)
    return {
        "activations": scatter_about(splits[0], (QUERIES, SEQ, D), 1.0, 6.0, ((0, 16), (2, 8))),
        "out_grads": scatter_about(splits[1], (QUERIES, SEQ, D), 1.0, 6.0, ((0, 16), (2, 8))),
        "proj_in": scatter_about(splits[2], (D, R), D ** -0.5, 0.0625, ((0, 8),)),
        "proj_out": scatter_about(splits[3], (D, R), D ** -0.5, 0.0625, ((0, 8),)),
        "lengths": draw_lengths(jax.random.fold_in(splits[7], 71), 0),
        "hess_tiles": draw_hess_tiles(jax.random.fold_in(splits[7], 71), 0),
        "train_grads": scatter_about(splits[6], (NTRAIN, FEATS), 1.0, 6.0, ((0, 16), (1, 8))),
    }


def reference(activations, out_grads, proj_in, proj_out, lengths, hess_tiles, train_grads):
    positions = jnp.arange(SEQ, dtype=jnp.int32)
    mask = (positions[None, :] < lengths[:, None]).astype(jnp.float32)[:, :, None]
    act_full = jnp.dot(activations.reshape(QUERIES * SEQ, D), proj_in, preferred_element_type=jnp.float32)
    grad_full = jnp.dot(out_grads.reshape(QUERIES * SEQ, D), proj_out, preferred_element_type=jnp.float32)
    act_low = (act_full.reshape(QUERIES, SEQ, R) * mask).astype(jnp.bfloat16)
    grad_low = (grad_full.reshape(QUERIES, SEQ, R) * mask).astype(jnp.bfloat16)
    kron = jnp.einsum('qti,qtj->qij', grad_low.astype(jnp.float32), act_low.astype(jnp.float32))
    kron = (kron * (1.0 / jnp.sqrt(jnp.float32(SEQ)))).astype(jnp.bfloat16)
    kron_blocks = kron.reshape(QUERIES, NBLK, BLK)
    precond = jnp.einsum('qbk,bkl->qbl', kron_blocks.astype(jnp.float32), hess_tiles.astype(jnp.float32))
    precond = precond.astype(jnp.bfloat16).reshape(QUERIES, FEATS)
    scores = lax.dot_general(precond, train_grads, (((1,), (1,)), ((), ())), preferred_element_type=jnp.float32)
    return scores * (1.0 / R)
```

```python
import jax
import jax.numpy as jnp
from jax import lax
from jax.experimental import pallas as pl
from jax.experimental.pallas import tpu as pltpu
from jax.sharding import PartitionSpec as P

MESH = pl.DeviceIdType.MESH
BF16 = jnp.bfloat16
F32 = jnp.float32
WAVES = 2
FEAT_PEERS = [(dz, dx) for dx in (1, 0) for dz in (2, 1, 3, 0) if (dz, dx) != (0, 0)]
ROW_PEERS = [(dx, dy) for dx in (1, 0) for dy in (2, 1, 3, 0) if (dx, dy) != (0, 0)]


def kernel(
    act, grad, proj_in, proj_out, lengths, hess, train, out,
    act_v, grad_v, pin_v, pout_v, hess_v, train_v,
    part_send, part_recv, part_own,
    kron_send, kron_recv, kron_f32, kron_lhs,
    gathered, score_f32, score_send, score_recv,
    load_sem, part_ss, part_rs, kron_ss, kron_rs,
    row_ss, row_rs, core_ss, core_rs, score_ss, score_rs,
):
    r = lax.axis_index("rows")
    f = lax.axis_index("feat")
    xh, y, c = r // 8, (r // 2) % 4, r % 2
    z, xl = f // 2, f % 2

    def feat_at(dz, dx):
        return lax.rem(z + dz, 4) * 2 + lax.rem(xl + dx, 2)

    def rows_at(dx, dy):
        return lax.rem(xh + dx, 2) * 8 + lax.rem(y + dy, 4) * 2 + c

    other_core = (r - c + (1 - c), f)

    loads = {}

    def load(key, src, dst, sem):
        loads[key] = pltpu.make_async_copy(src, dst, load_sem.at[sem])
        loads[key].start()

    load("pin", proj_in, pin_v, 0)
    load("pout", proj_out, pout_v, 1)
    barrier = pltpu.get_barrier_semaphore()
    targets = [(r, feat_at(*p)) for p in FEAT_PEERS]
    targets += [(rows_at(*p), f) for p in ROW_PEERS] + [other_core]
    for target in targets:
        pl.semaphore_signal(barrier, 1, device_id=target, device_id_type=MESH)
    sem = 4
    for w in range(WAVES):
        for k, p in enumerate(FEAT_PEERS + [(0, 0)]):
            row = pl.multiple_of((w * 16 + feat_at(*p) * 2) * 96, 192)
            load(("act", w, k), act.at[pl.ds(row, 192)], act_v.at[w, k], sem)
            load(("grad", w, k), grad.at[pl.ds(row, 192)], grad_v.at[w, k], sem + 1)
            sem += 2

    part_copies = {}
    for w in range(WAVES):
        for k, p in enumerate(FEAT_PEERS + [(0, 0)]):
            if w == 0 and k == 0:
                loads["pin"].wait()
                loads["pout"].wait()
            loads["act", w, k].wait()
            loads["grad", w, k].wait()
            a = jnp.dot(act_v[w, k], pin_v[...], preferred_element_type=F32)
            g = jnp.dot(grad_v[w, k], pout_v[...], preferred_element_type=F32)
            if k == len(FEAT_PEERS):
                part_own[w, :, 0:128] = a
                part_own[w, :, 128:256] = g
            else:
                part_send[w, k, :, 0:128] = a.astype(BF16)
                part_send[w, k, :, 128:256] = g.astype(BF16)
                if w == 0 and k == 0:
                    pl.semaphore_wait(barrier, len(targets))
                copy = pltpu.make_async_remote_copy(
                    part_send.at[w, k], part_recv.at[w, k],
                    part_ss.at[w, k], part_rs.at[w, k],
                    device_id=(r, feat_at(*p)), device_id_type=MESH,
                )
                if w > 0:
                    part_copies[w - 1, k].wait_send()
                copy.start()
                part_copies[w, k] = copy
        if w == 0:
            load("hess", hess, hess_v, 2)
    load("train", train, train_v, 3)

    n_feat = len(FEAT_PEERS)
    n_row = len(ROW_PEERS)
    sends = []

    def kron_stage(w):
        for k in range(n_feat):
            part_copies[w, k].wait_recv()
        total = part_own[w]
        for k in range(n_feat):
            total = total + part_recv[w, k].astype(F32)
        token = lax.broadcasted_iota(jnp.int32, (96, 256), 0)
        for q in range(2):
            length = lengths[w * 16 + f * 2 + q]
            both = jnp.where(token < length, total[q * 96:(q + 1) * 96], 0.0).astype(BF16)
            kron = lax.dot_general(
                both[:, 128:256], both[:, 0:128], (((0,), (0,)), ((), ())),
                preferred_element_type=F32,
            )
            kron = kron * (1.0 / jnp.sqrt(jnp.float32(96)))
            kron_send[w, :, q * 128:(q + 1) * 128] = kron.astype(BF16)
        copies = []
        for k, p in enumerate(FEAT_PEERS):
            target = feat_at(*p)
            copy = pltpu.make_async_remote_copy(
                kron_send.at[w, pl.ds(pl.multiple_of(target * 16, 16), 16)], kron_recv.at[w, f],
                kron_ss.at[w, k], kron_rs.at[w, k],
                device_id=(r, target), device_id_type=MESH,
            )
            copy.start()
            copies.append(copy)
        kron_recv[w, f] = kron_send[w, pl.ds(pl.multiple_of(f * 16, 16), 16)]
        return copies

    def precond_stage(w, copies):
        for copy in copies:
            copy.wait_recv()
            sends.append(copy)
        if w == 0:
            loads["hess"].wait()
        for s in range(8):
            for q in range(2):
                kron_f32[pl.ds((s * 2 + q) * 16, 16), :] = (
                    kron_recv[w, s, :, q * 128:(q + 1) * 128].astype(F32)
                )
        for i in range(16):
            kron_lhs[:, i * 128:(i + 1) * 128] = (
                kron_f32[pl.ds(i, 16, stride=16), :].astype(BF16)
            )
        for b in range(2):
            gathered[w, r, :, b * 1024:(b + 1) * 1024] = jnp.dot(
                kron_lhs[:, b * 1024:(b + 1) * 1024], hess_v[b], preferred_element_type=F32
            ).astype(BF16)
        copies = []
        for k, p in enumerate(ROW_PEERS):
            copy = pltpu.make_async_remote_copy(
                gathered.at[w, r], gathered.at[w, r], row_ss.at[w, k], row_rs.at[w, k],
                device_id=(rows_at(*p), f), device_id_type=MESH,
            )
            copy.start()
            copies.append(copy)
        return copies

    def forward(w, k, block):
        copy = pltpu.make_async_remote_copy(
            gathered.at[w, block], gathered.at[w, block], core_ss.at[w, k], core_rs.at[w, k],
            device_id=other_core, device_id_type=MESH,
        )
        copy.start()
        return copy

    def gather_stage(w, copies):
        forwards = [forward(w, n_row, r)]
        for k in (6, 4, 5, 2, 3, 1, 0):
            dx, dy = ROW_PEERS[k]
            copies[k].wait_recv()
            forwards.append(forward(w, k, rows_at(2 - dx, 4 - dy)))
        for copy in forwards:
            copy.wait_recv()
        sends.extend(copies)
        sends.extend(forwards)

    def score_stage(w):
        copies = []
        if w == 0:
            loads["train"].wait()
        for h in range(2):

            @pl.loop(0, 4)
            def _(n):
                col = pl.multiple_of(n * 256, 256)
                acc = lax.dot_general(
                    gathered[w].reshape(256, 2048),
                    train_v[pl.ds(pl.multiple_of(h * 1024 + col, 256), 256), :],
                    (((1,), (1,)), ((), ())), preferred_element_type=F32,
                )
                score_f32[w, h, :, pl.ds(col, 256)] = acc
                score_send[w, h, :, pl.ds(col, 256)] = acc.astype(BF16)

            for k, p in enumerate(FEAT_PEERS):
                target = feat_at(*p)
                copy = pltpu.make_async_remote_copy(
                    score_send.at[w, h, pl.ds(pl.multiple_of(target * 32, 32), 32)],
                    score_recv.at[w, h, k],
                    score_ss.at[w, h, k], score_rs.at[w, h, k],
                    device_id=(r, target), device_id_type=MESH,
                )
                copy.start()
                copies.append(copy)
        return copies

    def final_stage(w, copies):
        for h in range(2):
            for copy in copies[h * n_feat:(h + 1) * n_feat]:
                copy.wait_recv()
            total = score_f32[w, h, pl.ds(pl.multiple_of(f * 32, 32), 32), :]
            for k in range(n_feat):
                total = total + score_recv[w, h, k].astype(F32)
            total = total * (1.0 / 128)
            for core in range(2):
                out[pl.ds(core * 32 + w * 16, 16), pl.ds(h * 1024, 1024)] = (
                    total[core * 16:(core + 1) * 16]
                )
        sends.extend(copies)

    k0 = kron_stage(0)
    p0 = precond_stage(0, k0)
    gather_stage(0, p0)
    s0 = score_stage(0)
    k1 = kron_stage(1)
    p1 = precond_stage(1, k1)
    gather_stage(1, p1)
    s1 = score_stage(1)
    final_stage(0, s0)
    final_stage(1, s1)
    for k in range(n_feat):
        part_copies[WAVES - 1, k].wait_send()
    for copy in sends:
        copy.wait_send()


def on_device(activations, out_grads, proj_in, proj_out, lengths, hess_tiles, train_grads):
    hbm = pl.BlockSpec(memory_space=pl.ANY)
    n_feat, n_row = len(FEAT_PEERS), len(ROW_PEERS)
    dma = pltpu.SemaphoreType.DMA
    return pl.pallas_call(
        kernel,
        out_shape=jax.ShapeDtypeStruct((64, 2048), F32),
        in_specs=[hbm, hbm, hbm, hbm, pl.BlockSpec(memory_space=pltpu.SMEM), hbm, hbm],
        out_specs=pl.BlockSpec(memory_space=pltpu.VMEM),
        scratch_shapes=[
            pltpu.VMEM((WAVES, 8, 192, 1024), BF16),
            pltpu.VMEM((WAVES, 8, 192, 1024), BF16),
            pltpu.VMEM((1024, 128), BF16),
            pltpu.VMEM((1024, 128), BF16),
            pltpu.VMEM((2, 1024, 1024), BF16),
            pltpu.VMEM((2048, 2048), BF16),
            pltpu.VMEM((WAVES, n_feat, 192, 256), BF16),
            pltpu.VMEM((WAVES, n_feat, 192, 256), BF16),
            pltpu.VMEM((WAVES, 192, 256), F32),
            pltpu.VMEM((WAVES, 128, 256), BF16),
            pltpu.VMEM((WAVES, 8, 16, 256), BF16),
            pltpu.VMEM((256, 128), F32),
            pltpu.VMEM((16, 2048), BF16),
            pltpu.VMEM((WAVES, 16, 16, 2048), BF16),
            pltpu.VMEM((WAVES, 2, 256, 1024), F32),
            pltpu.VMEM((WAVES, 2, 256, 1024), BF16),
            pltpu.VMEM((WAVES, 2, n_feat, 32, 1024), BF16),
            dma((4 + WAVES * 16,)),
            dma((WAVES, n_feat)), dma((WAVES, n_feat)),
            dma((WAVES, n_feat)), dma((WAVES, n_feat)),
            dma((WAVES, n_row)), dma((WAVES, n_row)),
            dma((WAVES, n_row + 1)), dma((WAVES, n_row + 1)),
            dma((WAVES, 2, n_feat)), dma((WAVES, 2, n_feat)),
        ],
        compiler_params=pltpu.CompilerParams(
            collective_id=0, has_side_effects=True, vmem_limit_bytes=56 * 1024 * 1024
        ),
        cost_estimate=pl.CostEstimate(
            flops=6_000_000_000, bytes_accessed=26_000_000, transcendentals=0
        ),
        name="influence",
    )(
        activations.reshape(3072, 1024), out_grads.reshape(3072, 1024),
        proj_in, proj_out, lengths, hess_tiles, train_grads,
    )


def solution(mesh):
    return jax.shard_map(
        on_device,
        mesh=mesh,
        in_specs=(
            P("rows", None, "feat"),
            P("rows", None, "feat"),
            P("feat", None),
            P("feat", None),
            P("rows"),
            P("feat", None, None),
            P("rows", "feat"),
        ),
        out_specs=P("feat", "rows"),
        check_vma=False,
    )
```

```python
import jax
import jax.numpy as jnp
from jax import lax
from jax.experimental import pallas as pl
from jax.experimental.pallas import tpu as pltpu
from jax.sharding import PartitionSpec as P

MESH = pl.DeviceIdType.MESH
BF16 = jnp.bfloat16
F32 = jnp.float32
WAVES = 2
NTILE = 512
FEAT_PEERS = [(dz, dx) for dx in (1, 0) for dz in (2, 1, 3, 0) if (dz, dx) != (0, 0)]
ROW_PEERS = [(dx, dy) for dx in (1, 0) for dy in (2, 1, 3, 0) if (dx, dy) != (0, 0)]
PART_ORDER = [
    ("grad", 2, 0), ("grad", 2, 1), ("act", 2, 1), ("grad", 1, 0), ("grad", 1, 1), ("act", 1, 1),
    ("grad", 3, 0), ("grad", 3, 1), ("act", 3, 1), ("act", 0, 1),
    ("grad", 0, 1), ("act", 2, 0), ("act", 1, 0), ("act", 3, 0), ("grad", 0, 0), ("act", 0, 0),
]


def kernel(
    act, grad, proj_in, proj_out, lengths_hbm, hess, train, out,
    lengths,
    act_v, grad_v, pin_v, pout_v, hess_v, train_v,
    a_send, a_recv, a_own, a_sum, a_recv2,
    g_send, g_recv, g_own, g_sum, g_recv2,
    kron_send, kron_recv, kron_f32, kron_lhs,
    gathered, score_f32, score_send, x_recv, x_sum, x_recv2, z_recv, z_sum, z_recv2,
    load_sem, a_ss, a_rs, g_ss, g_rs, kron_ss, kron_rs,
    row_ss, row_rs, core_ss, core_rs, xs_ss, xs_rs, zs_ss, zs_rs,
):
    r = lax.axis_index("rows")
    f = lax.axis_index("feat")
    xh, y, c = r // 8, (r // 2) % 4, r % 2
    z, xl = f // 2, f % 2

    def feat_at(dz, dx):
        return lax.rem(z + dz, 4) * 2 + lax.rem(xl + dx, 2)

    def rows_at(dx, dy):
        return lax.rem(xh + dx, 2) * 8 + lax.rem(y + dy, 4) * 2 + c

    other_core = (r - c + (1 - c), f)
    sends = []

    def send(src, dst, ssem, rsem, target):
        copy = pltpu.make_async_remote_copy(
            src, dst, ssem, rsem, device_id=target, device_id_type=MESH
        )
        copy.start()
        sends.append(copy)
        return copy

    loads = {}

    def load(key, src, dst, sem):
        loads[key] = pltpu.make_async_copy(src, dst, load_sem.at[sem])
        loads[key].start()

    load("pin", proj_in, pin_v, 0)
    load("pout", proj_out, pout_v, 1)
    load("lengths", lengths_hbm, lengths, 4 + WAVES * 16)
    barrier = pltpu.get_barrier_semaphore()
    targets = [(r, feat_at(*p)) for p in FEAT_PEERS]
    targets += [(rows_at(*p), f) for p in ROW_PEERS] + [other_core]
    for target in targets:
        pl.semaphore_signal(barrier, 1, device_id=target, device_id_type=MESH)
    for w in range(WAVES):
        for k, (which, dz, dx) in enumerate(PART_ORDER):
            row = pl.multiple_of((w * 16 + feat_at(dz, dx) * 2) * 96, 192)
            src, dst = (act, act_v) if which == "act" else (grad, grad_v)
            load(
                (w, which, dz, dx), src.at[pl.ds(row, 192)], dst.at[w, dz * 2 + dx],
                4 + w * 16 + k,
            )

    a_copies, g_copies = {}, {}
    for w in range(WAVES):
        for k, (which, dz, dx) in enumerate(PART_ORDER):
            if w == 0 and k == 0:
                loads["pin"].wait()
                loads["pout"].wait()
            loads[w, which, dz, dx].wait()
            if which == "act":
                part = jnp.dot(act_v[w, dz * 2 + dx], pin_v[...], preferred_element_type=F32)
                if dx == 0:
                    a_own[w, dz] = part
                    continue
                a_send[w, dz] = part.astype(BF16)
            else:
                part = jnp.dot(grad_v[w, dz * 2 + dx], pout_v[...], preferred_element_type=F32)
                if dz == 0:
                    g_own[w, dx] = part
                    continue
                g_send[w, dz - 1, dx] = part.astype(BF16)
                if dx == 0:
                    continue
            if w == 0 and k == 1:
                pl.semaphore_wait(barrier, len(targets))
            if which == "act":
                a_copies[w, dz] = send(
                    a_send.at[w, dz], a_recv.at[w, dz], a_ss.at[w, dz], a_rs.at[w, dz],
                    (r, feat_at(0, 1)),
                )
            else:
                g_copies[w, dz] = send(
                    g_send.at[w, dz - 1], g_recv.at[w, dz - 1], g_ss.at[w, dz], g_rs.at[w, dz],
                    (r, feat_at(dz, 0)),
                )
        if w == 0:
            load("hess", hess, hess_v, 2)
    load("train", train, train_v, 3)

    def part_stage(w):
        for dz in (2, 1, 3):
            a_copies[w, dz].wait_recv()
            a_sum[w, dz - 1] = (a_own[w, dz] + a_recv[w, dz].astype(F32)).astype(BF16)
            a_copies[w, 3 + dz] = send(
                a_sum.at[w, dz - 1], a_recv2.at[w, dz - 1],
                a_ss.at[w, 3 + dz], a_rs.at[w, 3 + dz], (r, feat_at(dz, 0)),
            )
        for dz in (2, 1, 3):
            g_copies[w, dz].wait_recv()
        g_sum[w] = (
            g_own[w, 1] + g_recv[w, 0, 1].astype(F32)
            + g_recv[w, 1, 1].astype(F32) + g_recv[w, 2, 1].astype(F32)
        ).astype(BF16)
        g_copies[w, 0] = send(
            g_sum.at[w], g_recv2.at[w], g_ss.at[w, 0], g_rs.at[w, 0], (r, feat_at(0, 1))
        )

    def kron_stage(w):
        a_copies[w, 0].wait_recv()
        for dz in (1, 2, 3):
            a_copies[w, 3 + dz].wait_recv()
        g_copies[w, 0].wait_recv()
        low_a = a_own[w, 0] + a_recv[w, 0].astype(F32)
        low_g = g_own[w, 0] + g_recv2[w].astype(F32)
        for dz in range(3):
            low_a = low_a + a_recv2[w, dz].astype(F32)
            low_g = low_g + g_recv[w, dz, 0].astype(F32)
        if w == 0:
            loads["lengths"].wait()
        token = lax.broadcasted_iota(jnp.int32, (96, 128), 0)
        for q in range(2):
            length = lengths[w * 16 + f * 2 + q]
            a = jnp.where(token < length, low_a[q * 96:(q + 1) * 96], 0.0)
            g = jnp.where(token < length, low_g[q * 96:(q + 1) * 96], 0.0)
            a_hi, g_hi = a.astype(BF16), g.astype(BF16)
            a_lo, g_lo = (a - a_hi.astype(F32)).astype(BF16), (g - g_hi.astype(F32)).astype(BF16)

            def outer(left, right):
                return lax.dot_general(
                    left, right, (((0,), (0,)), ((), ())), preferred_element_type=F32
                )

            kron = outer(g_hi, a_hi) + outer(g_hi, a_lo) + outer(g_lo, a_hi)
            kron = kron * (1.0 / jnp.sqrt(jnp.float32(96)))
            kron_send[w, :, q * 128:(q + 1) * 128] = kron.astype(BF16)
        copies = []
        for k, p in enumerate(FEAT_PEERS):
            target = feat_at(*p)
            copies.append(send(
                kron_send.at[w, pl.ds(pl.multiple_of(target * 16, 16), 16)], kron_recv.at[w, f],
                kron_ss.at[w, k], kron_rs.at[w, k], (r, target),
            ))
        kron_recv[w, f] = kron_send[w, pl.ds(pl.multiple_of(f * 16, 16), 16)]
        return copies

    def precond_stage(w, copies):
        for copy in copies:
            copy.wait_recv()
        if w == 0:
            loads["hess"].wait()
        for s in range(8):
            for q in range(2):
                kron_f32[pl.ds((s * 2 + q) * 16, 16), :] = (
                    kron_recv[w, s, :, q * 128:(q + 1) * 128].astype(F32)
                )
        for i in range(16):
            kron_lhs[:, i * 128:(i + 1) * 128] = (
                kron_f32[pl.ds(i, 16, stride=16), :].astype(BF16)
            )
        for b in range(2):
            gathered[w, r, :, b * 1024:(b + 1) * 1024] = jnp.dot(
                kron_lhs[:, b * 1024:(b + 1) * 1024], hess_v[b], preferred_element_type=F32
            ).astype(BF16)
        return [
            send(
                gathered.at[w, r], gathered.at[w, r], row_ss.at[w, k], row_rs.at[w, k],
                (rows_at(*p), f),
            )
            for k, p in enumerate(ROW_PEERS)
        ] + [forward(w, len(ROW_PEERS), r)]

    def forward(w, k, block):
        return send(
            gathered.at[w, block], gathered.at[w, block], core_ss.at[w, k], core_rs.at[w, k],
            other_core,
        )

    def gather_stage(w, copies):
        forwards = [copies[-1]]
        for k in (6, 4, 5, 2, 3, 1, 0):
            dx, dy = ROW_PEERS[k]
            copies[k].wait_recv()
            forwards.append(forward(w, k, rows_at(2 - dx, 4 - dy)))
        for copy in forwards:
            copy.wait_recv()

    def score_matmul(w, h):
        @pl.loop(0, 1024 // NTILE)
        def _(n):
            col = pl.multiple_of(n * NTILE, NTILE)
            acc = lax.dot_general(
                gathered[w].reshape(256, 2048),
                train_v[pl.ds(pl.multiple_of(h * 1024 + col, NTILE), NTILE), :],
                (((1,), (1,)), ((), ())), preferred_element_type=F32,
            )
            score_f32[w, h, :, pl.ds(col, NTILE)] = acc
            score_send[w, h, :, pl.ds(col, NTILE)] = acc.astype(BF16)

    def rows_for(target, count=32):
        return pl.ds(pl.multiple_of(target * count, count), count)

    xs, zs = {}, {}

    def score_stage(w):
        if w == 0:
            loads["train"].wait()
        score_matmul(w, 0)
        for dz in (2, 1, 3, 0):
            xs[w, dz] = send(
                score_send.at[w, 0, rows_for(feat_at(dz, 1))], x_recv.at[w, dz],
                xs_ss.at[w, dz], xs_rs.at[w, dz], (r, feat_at(0, 1)),
            )
        score_matmul(w, 1)
        for dz in (2, 1, 3):
            zs[w, dz] = send(
                score_send.at[w, 1, rows_for(lax.rem(z + dz, 4), 64)], z_recv.at[w, dz - 1],
                zs_ss.at[w, dz], zs_rs.at[w, dz], (r, feat_at(dz, 0)),
            )

    def score_stage2(w):
        for dz in (2, 1, 3):
            xs[w, dz].wait_recv()
            x_sum[w, dz - 1] = (
                score_f32[w, 0, rows_for(feat_at(dz, 0)), :] + x_recv[w, dz].astype(F32)
            ).astype(BF16)
            xs[w, 3 + dz] = send(
                x_sum.at[w, dz - 1], x_recv2.at[w, dz - 1],
                xs_ss.at[w, 3 + dz], xs_rs.at[w, 3 + dz], (r, feat_at(dz, 0)),
            )
        for dz in (2, 1, 3):
            zs[w, dz].wait_recv()
        total = score_f32[w, 1, rows_for(feat_at(0, 1)), :]
        for dz in range(3):
            total = total + z_recv[w, dz, rows_for(1 - xl), :].astype(F32)
        z_sum[w] = total.astype(BF16)
        zs[w, 0] = send(
            z_sum.at[w], z_recv2.at[w], zs_ss.at[w, 0], zs_rs.at[w, 0], (r, feat_at(0, 1))
        )

    def final_stage(w):
        xs[w, 0].wait_recv()
        for dz in (1, 2, 3):
            xs[w, 3 + dz].wait_recv()
        zs[w, 0].wait_recv()
        first = score_f32[w, 0, rows_for(f), :] + x_recv[w, 0].astype(F32)
        second = score_f32[w, 1, rows_for(f), :] + z_recv2[w].astype(F32)
        for dz in range(3):
            first = first + x_recv2[w, dz].astype(F32)
            second = second + z_recv[w, dz, rows_for(xl), :].astype(F32)
        for core in range(2):
            rows = pl.ds(core * 32 + w * 16, 16)
            out[rows, 0:1024] = first[core * 16:(core + 1) * 16] * (1.0 / 128)
            out[rows, 1024:2048] = second[core * 16:(core + 1) * 16] * (1.0 / 128)

    part_stage(0)
    part_stage(1)
    k0 = kron_stage(0)
    k1 = kron_stage(1)
    p0 = precond_stage(0, k0)
    p1 = precond_stage(1, k1)
    gather_stage(0, p0)
    score_stage(0)
    gather_stage(1, p1)
    score_stage(1)
    score_stage2(0)
    score_stage2(1)
    final_stage(0)
    final_stage(1)
    for copy in sends:
        copy.wait_send()


def on_device(activations, out_grads, proj_in, proj_out, lengths, hess_tiles, train_grads):
    hbm = pl.BlockSpec(memory_space=pl.ANY)
    n_feat, n_row = len(FEAT_PEERS), len(ROW_PEERS)
    dma = pltpu.SemaphoreType.DMA
    return pl.pallas_call(
        kernel,
        out_shape=jax.ShapeDtypeStruct((64, 2048), F32),
        in_specs=[hbm, hbm, hbm, hbm, hbm, hbm, hbm],
        out_specs=pl.BlockSpec(memory_space=pltpu.VMEM),
        scratch_shapes=[
            pltpu.SMEM((32,), jnp.int32),
            pltpu.VMEM((WAVES, 8, 192, 1024), BF16),
            pltpu.VMEM((WAVES, 8, 192, 1024), BF16),
            pltpu.VMEM((1024, 128), BF16),
            pltpu.VMEM((1024, 128), BF16),
            pltpu.VMEM((2, 1024, 1024), BF16),
            pltpu.VMEM((2048, 2048), BF16),
            pltpu.VMEM((WAVES, 4, 192, 128), BF16),
            pltpu.VMEM((WAVES, 4, 192, 128), BF16),
            pltpu.VMEM((WAVES, 4, 192, 128), F32),
            pltpu.VMEM((WAVES, 3, 192, 128), BF16),
            pltpu.VMEM((WAVES, 3, 192, 128), BF16),
            pltpu.VMEM((WAVES, 3, 2, 192, 128), BF16),
            pltpu.VMEM((WAVES, 3, 2, 192, 128), BF16),
            pltpu.VMEM((WAVES, 2, 192, 128), F32),
            pltpu.VMEM((WAVES, 192, 128), BF16),
            pltpu.VMEM((WAVES, 192, 128), BF16),
            pltpu.VMEM((WAVES, 128, 256), BF16),
            pltpu.VMEM((WAVES, 8, 16, 256), BF16),
            pltpu.VMEM((256, 128), F32),
            pltpu.VMEM((16, 2048), BF16),
            pltpu.VMEM((WAVES, 16, 16, 2048), BF16),
            pltpu.VMEM((WAVES, 2, 256, 1024), F32),
            pltpu.VMEM((WAVES, 2, 256, 1024), BF16),
            pltpu.VMEM((WAVES, 4, 32, 1024), BF16),
            pltpu.VMEM((WAVES, 3, 32, 1024), BF16),
            pltpu.VMEM((WAVES, 3, 32, 1024), BF16),
            pltpu.VMEM((WAVES, 3, 64, 1024), BF16),
            pltpu.VMEM((WAVES, 32, 1024), BF16),
            pltpu.VMEM((WAVES, 32, 1024), BF16),
            dma((5 + WAVES * 16,)),
            dma((WAVES, 7)), dma((WAVES, 7)),
            dma((WAVES, 4)), dma((WAVES, 4)),
            dma((WAVES, n_feat)), dma((WAVES, n_feat)),
            dma((WAVES, n_row)), dma((WAVES, n_row)),
            dma((WAVES, n_row + 1)), dma((WAVES, n_row + 1)),
            dma((WAVES, 7)), dma((WAVES, 7)),
            dma((WAVES, 4)), dma((WAVES, 4)),
        ],
        compiler_params=pltpu.CompilerParams(
            collective_id=0, has_side_effects=True, vmem_limit_bytes=56 * 1024 * 1024
        ),
        cost_estimate=pl.CostEstimate(
            flops=6_000_000_000, bytes_accessed=26_000_000, transcendentals=0
        ),
        name="influence",
    )(
        activations.reshape(3072, 1024), out_grads.reshape(3072, 1024),
        proj_in, proj_out, lengths, hess_tiles, train_grads,
    )


def solution(mesh):
    return jax.shard_map(
        on_device,
        mesh=mesh,
        in_specs=(
            P("rows", None, "feat"),
            P("rows", None, "feat"),
            P("feat", None),
            P("feat", None),
            P("rows"),
            P("feat", None, None),
            P("rows", "feat"),
        ),
        out_specs=P("feat", "rows"),
        check_vma=False,
    )
```

```python
import jax
import jax.numpy as jnp
from jax import lax
from jax.experimental import pallas as pl
from jax.experimental.pallas import tpu as pltpu
from jax.sharding import PartitionSpec as P

MESH = pl.DeviceIdType.MESH
BF16 = jnp.bfloat16
F32 = jnp.float32
WAVES = 2
FEAT_PEERS = [(dz, dx) for dx in (1, 0) for dz in (2, 1, 3, 0) if (dz, dx) != (0, 0)]
ROW_PEERS = [(1, 0), (0, 2), (0, 1), (0, 3)]
PART_ORDER = [
    ("grad", 2, 0), ("grad", 2, 1), ("act", 2, 1), ("grad", 1, 0), ("grad", 1, 1), ("act", 1, 1),
    ("grad", 3, 0), ("grad", 3, 1), ("act", 3, 1), ("act", 0, 1),
    ("grad", 0, 1), ("act", 2, 0), ("act", 1, 0), ("act", 3, 0), ("grad", 0, 0), ("act", 0, 0),
]


def kernel(
    act, grad, proj_in, proj_out, lengths_hbm, hess, train, out,
    lengths,
    act_v, grad_v, pin_v, pout_v, hess_v, train_v,
    a_send, a_recv, a_own, a_sum, a_recv2,
    g_send, g_recv, g_own, g_sum, g_recv2,
    kron_send, kron_recv, kron_f32, kron_lhs,
    gathered, score_f32, score_send, x_recv, x_sum, x_recv2, z_recv, z_sum, z_recv2,
    load_sem, a_ss, a_rs, g_ss, g_rs, kron_ss, kron_rs,
    row_ss, row_rs, core_ss, core_rs, xs_ss, xs_rs, zs_ss, zs_rs,
):
    r = lax.axis_index("rows")
    f = lax.axis_index("feat")
    xh, y, c = r // 8, (r // 2) % 4, r % 2
    z, xl = f // 2, f % 2

    def feat_at(dz, dx):
        return lax.rem(z + dz, 4) * 2 + lax.rem(xl + dx, 2)

    def rows_at(dx, dy):
        return lax.rem(xh + dx, 2) * 8 + lax.rem(y + dy, 4) * 2 + c

    other_core = (r - c + (1 - c), f)
    sends = []

    def send(src, dst, ssem, rsem, target):
        copy = pltpu.make_async_remote_copy(
            src, dst, ssem, rsem, device_id=target, device_id_type=MESH
        )
        copy.start()
        sends.append(copy)
        return copy

    barrier = pltpu.get_barrier_semaphore()
    targets = [(r, feat_at(*p)) for p in FEAT_PEERS]
    targets += [(rows_at(*p), f) for p in ROW_PEERS] + [other_core]
    for target in targets:
        pl.semaphore_signal(barrier, 1, device_id=target, device_id_type=MESH)

    loads = {}

    def load(key, src, dst, sem):
        loads[key] = pltpu.make_async_copy(src, dst, load_sem.at[sem])
        loads[key].start()

    load("pin", proj_in, pin_v, 0)
    load("pout", proj_out, pout_v, 1)
    load("lengths", lengths_hbm, lengths, 4 + WAVES * 16)
    for w in range(WAVES):
        for k, (which, dz, dx) in enumerate(PART_ORDER):
            row = pl.multiple_of((w * 16 + feat_at(dz, dx) * 2) * 96, 192)
            src, dst = (act, act_v) if which == "act" else (grad, grad_v)
            load(
                (w, which, dz, dx), src.at[pl.ds(row, 192)], dst.at[w, dz * 2 + dx],
                4 + w * 16 + k,
            )

    a_copies, g_copies = {}, {}
    for w in range(WAVES):
        for k, (which, dz, dx) in enumerate(PART_ORDER):
            if w == 0 and k == 0:
                loads["pin"].wait()
                loads["pout"].wait()
            loads[w, which, dz, dx].wait()
            if which == "act":
                part = jnp.dot(act_v[w, dz * 2 + dx], pin_v[...], preferred_element_type=F32)
                if dx == 0:
                    a_own[w, dz] = part
                    continue
                a_send[w, dz] = part.astype(BF16)
            else:
                part = jnp.dot(grad_v[w, dz * 2 + dx], pout_v[...], preferred_element_type=F32)
                if dz == 0:
                    g_own[w, dx] = part
                    continue
                g_send[w, dz - 1, dx] = part.astype(BF16)
                if dx == 0:
                    continue
            if w == 0 and k == 1:
                pl.semaphore_wait(barrier, len(targets))
            if w > 0:
                earlier = (a_copies if which == "act" else g_copies)[w - 1, dz]
                earlier.wait_send()
                sends[:] = [copy for copy in sends if copy is not earlier]
            if which == "act":
                a_copies[w, dz] = send(
                    a_send.at[w, dz], a_recv.at[w, dz], a_ss.at[w, dz], a_rs.at[w, dz],
                    (r, feat_at(0, 1)),
                )
            else:
                g_copies[w, dz] = send(
                    g_send.at[w, dz - 1], g_recv.at[w, dz - 1], g_ss.at[w, dz], g_rs.at[w, dz],
                    (r, feat_at(dz, 0)),
                )
        if w == 0:
            load("hess", hess, hess_v, 2)
    load("train", train, train_v, 3)

    def part_stage(w):
        for dz in (2, 1, 3):
            a_copies[w, dz].wait_recv()
            a_sum[w, dz - 1] = (a_own[w, dz] + a_recv[w, dz].astype(F32)).astype(BF16)
            a_copies[w, 3 + dz] = send(
                a_sum.at[w, dz - 1], a_recv2.at[w, dz - 1],
                a_ss.at[w, 3 + dz], a_rs.at[w, 3 + dz], (r, feat_at(dz, 0)),
            )
        for dz in (2, 1, 3):
            g_copies[w, dz].wait_recv()
        g_sum[w] = (
            g_own[w, 1] + g_recv[w, 0, 1].astype(F32)
            + g_recv[w, 1, 1].astype(F32) + g_recv[w, 2, 1].astype(F32)
        ).astype(BF16)
        g_copies[w, 0] = send(
            g_sum.at[w], g_recv2.at[w], g_ss.at[w, 0], g_rs.at[w, 0], (r, feat_at(0, 1))
        )

    def kron_stage(w):
        a_copies[w, 0].wait_recv()
        for dz in (1, 2, 3):
            a_copies[w, 3 + dz].wait_recv()
        g_copies[w, 0].wait_recv()
        low_a = a_own[w, 0] + a_recv[w, 0].astype(F32)
        low_g = g_own[w, 0] + g_recv2[w].astype(F32)
        for dz in range(3):
            low_a = low_a + a_recv2[w, dz].astype(F32)
            low_g = low_g + g_recv[w, dz, 0].astype(F32)
        if w == 0:
            loads["lengths"].wait()
        token = lax.broadcasted_iota(jnp.int32, (96, 128), 0)
        for q in range(2):
            length = lengths[w * 16 + f * 2 + q]
            a = jnp.where(token < length, low_a[q * 96:(q + 1) * 96], 0.0)
            g = jnp.where(token < length, low_g[q * 96:(q + 1) * 96], 0.0)
            a_hi, g_hi = a.astype(BF16), g.astype(BF16)
            a_lo, g_lo = (a - a_hi.astype(F32)).astype(BF16), (g - g_hi.astype(F32)).astype(BF16)

            def outer(left, right):
                return lax.dot_general(
                    left, right, (((0,), (0,)), ((), ())), preferred_element_type=F32
                )

            kron = outer(g_hi, a_hi) + outer(g_hi, a_lo) + outer(g_lo, a_hi)
            kron = kron * (1.0 / jnp.sqrt(jnp.float32(96)))
            kron_send[w, :, q * 128:(q + 1) * 128] = kron.astype(BF16)
        copies = []
        for k, p in enumerate(FEAT_PEERS):
            target = feat_at(*p)
            copies.append(send(
                kron_send.at[w, pl.ds(pl.multiple_of(target * 16, 16), 16)], kron_recv.at[w, f],
                kron_ss.at[w, k], kron_rs.at[w, k], (r, target),
            ))
        kron_recv[w, f] = kron_send[w, pl.ds(pl.multiple_of(f * 16, 16), 16)]
        return copies

    def precond_stage(w, copies):
        for copy in copies:
            copy.wait_recv()
        if w == 0:
            loads["hess"].wait()
        for s in range(8):
            for q in range(2):
                kron_f32[pl.ds((s * 2 + q) * 16, 16), :] = (
                    kron_recv[w, s, :, q * 128:(q + 1) * 128].astype(F32)
                )
        for i in range(16):
            kron_lhs[:, i * 128:(i + 1) * 128] = (
                kron_f32[pl.ds(i, 16, stride=16), :].astype(BF16)
            )
        for b in range(2):
            gathered[w, r, :, b * 1024:(b + 1) * 1024] = jnp.dot(
                kron_lhs[:, b * 1024:(b + 1) * 1024], hess_v[b], preferred_element_type=F32
            ).astype(BF16)

    def share(w, block, k, target):
        return send(
            gathered.at[w, block], gathered.at[w, block], row_ss.at[w, k], row_rs.at[w, k], target
        )

    def forward(w, k, block):
        return send(
            gathered.at[w, block], gathered.at[w, block], core_ss.at[w, k], core_rs.at[w, k],
            other_core,
        )

    def share_stage(w):
        copies = {"x": share(w, r, 0, (rows_at(1, 0), f))}
        for dy in (2, 1, 3):
            copies[0, dy] = share(w, r, dy, (rows_at(0, dy), f))
        return copies, [forward(w, 0, r)]

    def relay_stage(w, copies, forwards):
        copies["x"].wait_recv()
        for dy in (2, 1, 3):
            copies[1, dy] = share(w, rows_at(1, 0), 3 + dy, (rows_at(0, dy), f))
        forwards.append(forward(w, 4, rows_at(1, 0)))

    def gather_stage(w, copies, forwards):
        for dx in range(2):
            for dy in (1, 3, 2):
                copies[dx, dy].wait_recv()
                forwards.append(forward(w, dx * 4 + dy, rows_at(dx, 4 - dy)))
        for copy in forwards:
            copy.wait_recv()

    def rows_for(target, count=32):
        return pl.ds(pl.multiple_of(target * count, count), count)

    def score_matmul(w, block):
        acc = lax.dot_general(
            gathered[w].reshape(256, 2048), train_v[block * 512:(block + 1) * 512, :],
            (((1,), (1,)), ((), ())), preferred_element_type=F32,
        )
        score_f32[w, block] = acc
        score_send[w, block] = acc.astype(BF16)

    xs, zs = {}, {}

    def score_stage(w):
        if w == 0:
            loads["train"].wait()
        for s in range(2):
            score_matmul(w, s)
            for dz in (2, 1, 3, 0):
                xs[w, s, dz] = send(
                    score_send.at[w, s, rows_for(feat_at(dz, 1))], x_recv.at[w, s, dz],
                    xs_ss.at[w, s, dz], xs_rs.at[w, s, dz], (r, feat_at(0, 1)),
                )
            score_matmul(w, 2 + s)
            for dz in (2, 1, 3):
                zs[w, s, dz] = send(
                    score_send.at[w, 2 + s, rows_for(lax.rem(z + dz, 4), 64)],
                    z_recv.at[w, s, dz - 1],
                    zs_ss.at[w, s, dz], zs_rs.at[w, s, dz], (r, feat_at(dz, 0)),
                )

    def score_stage2(w, s):
        for dz in (2, 1, 3):
            xs[w, s, dz].wait_recv()
            x_sum[w, s, dz - 1] = (
                score_f32[w, s, rows_for(feat_at(dz, 0)), :] + x_recv[w, s, dz].astype(F32)
            ).astype(BF16)
            xs[w, s, 3 + dz] = send(
                x_sum.at[w, s, dz - 1], x_recv2.at[w, s, dz - 1],
                xs_ss.at[w, s, 3 + dz], xs_rs.at[w, s, 3 + dz], (r, feat_at(dz, 0)),
            )
        for dz in (2, 1, 3):
            zs[w, s, dz].wait_recv()
        total = score_f32[w, 2 + s, rows_for(feat_at(0, 1)), :]
        for dz in range(3):
            total = total + z_recv[w, s, dz, rows_for(1 - xl), :].astype(F32)
        z_sum[w, s] = total.astype(BF16)
        zs[w, s, 0] = send(
            z_sum.at[w, s], z_recv2.at[w, s], zs_ss.at[w, s, 0], zs_rs.at[w, s, 0],
            (r, feat_at(0, 1)),
        )

    def final_stage(w, s):
        xs[w, s, 0].wait_recv()
        for dz in (1, 2, 3):
            xs[w, s, 3 + dz].wait_recv()
        zs[w, s, 0].wait_recv()
        first = score_f32[w, s, rows_for(f), :] + x_recv[w, s, 0].astype(F32)
        second = score_f32[w, 2 + s, rows_for(f), :] + z_recv2[w, s].astype(F32)
        for dz in range(3):
            first = first + x_recv2[w, s, dz].astype(F32)
            second = second + z_recv[w, s, dz, rows_for(xl), :].astype(F32)
        for core in range(2):
            rows = pl.ds(core * 32 + w * 16, 16)
            half = slice(core * 16, (core + 1) * 16)
            out[rows, s * 512:(s + 1) * 512] = first[half] * (1.0 / 128)
            out[rows, 1024 + s * 512:1536 + s * 512] = second[half] * (1.0 / 128)

    part_stage(0)
    k0 = kron_stage(0)
    part_stage(1)
    precond_stage(0, k0)
    g0 = share_stage(0)
    k1 = kron_stage(1)
    precond_stage(1, k1)
    relay_stage(0, *g0)
    g1 = share_stage(1)
    relay_stage(1, *g1)
    gather_stage(0, *g0)
    score_stage(0)
    gather_stage(1, *g1)
    score_stage(1)
    for w in range(WAVES):
        for s in range(2):
            score_stage2(w, s)
    for w in range(WAVES):
        for s in range(2):
            final_stage(w, s)
    for copy in sends:
        copy.wait_send()


def on_device(activations, out_grads, proj_in, proj_out, lengths, hess_tiles, train_grads):
    hbm = pl.BlockSpec(memory_space=pl.ANY)
    n_feat = len(FEAT_PEERS)
    dma = pltpu.SemaphoreType.DMA
    return pl.pallas_call(
        kernel,
        out_shape=jax.ShapeDtypeStruct((64, 2048), F32),
        in_specs=[hbm, hbm, hbm, hbm, hbm, hbm, hbm],
        out_specs=pl.BlockSpec(memory_space=pltpu.VMEM),
        scratch_shapes=[
            pltpu.SMEM((32,), jnp.int32),
            pltpu.VMEM((WAVES, 8, 192, 1024), BF16),
            pltpu.VMEM((WAVES, 8, 192, 1024), BF16),
            pltpu.VMEM((1024, 128), BF16),
            pltpu.VMEM((1024, 128), BF16),
            pltpu.VMEM((2, 1024, 1024), BF16),
            pltpu.VMEM((2048, 2048), BF16),
            pltpu.VMEM((WAVES, 4, 192, 128), BF16),
            pltpu.VMEM((WAVES, 4, 192, 128), BF16),
            pltpu.VMEM((WAVES, 4, 192, 128), F32),
            pltpu.VMEM((WAVES, 3, 192, 128), BF16),
            pltpu.VMEM((WAVES, 3, 192, 128), BF16),
            pltpu.VMEM((WAVES, 3, 2, 192, 128), BF16),
            pltpu.VMEM((WAVES, 3, 2, 192, 128), BF16),
            pltpu.VMEM((WAVES, 2, 192, 128), F32),
            pltpu.VMEM((WAVES, 192, 128), BF16),
            pltpu.VMEM((WAVES, 192, 128), BF16),
            pltpu.VMEM((WAVES, 128, 256), BF16),
            pltpu.VMEM((WAVES, 8, 16, 256), BF16),
            pltpu.VMEM((256, 128), F32),
            pltpu.VMEM((16, 2048), BF16),
            pltpu.VMEM((WAVES, 16, 16, 2048), BF16),
            pltpu.VMEM((WAVES, 4, 256, 512), F32),
            pltpu.VMEM((WAVES, 4, 256, 512), BF16),
            pltpu.VMEM((WAVES, 2, 4, 32, 512), BF16),
            pltpu.VMEM((WAVES, 2, 3, 32, 512), BF16),
            pltpu.VMEM((WAVES, 2, 3, 32, 512), BF16),
            pltpu.VMEM((WAVES, 2, 3, 64, 512), BF16),
            pltpu.VMEM((WAVES, 2, 32, 512), BF16),
            pltpu.VMEM((WAVES, 2, 32, 512), BF16),
            dma((5 + WAVES * 16,)),
            dma((WAVES, 7)), dma((WAVES, 7)),
            dma((WAVES, 4)), dma((WAVES, 4)),
            dma((WAVES, n_feat)), dma((WAVES, n_feat)),
            dma((WAVES, 7)), dma((WAVES, 7)),
            dma((WAVES, 8)), dma((WAVES, 8)),
            dma((WAVES, 2, 7)), dma((WAVES, 2, 7)),
            dma((WAVES, 2, 4)), dma((WAVES, 2, 4)),
        ],
        compiler_params=pltpu.CompilerParams(
            collective_id=0, has_side_effects=True, vmem_limit_bytes=56 * 1024 * 1024
        ),
        cost_estimate=pl.CostEstimate(
            flops=6_000_000_000, bytes_accessed=26_000_000, transcendentals=0
        ),
        name="influence",
    )(
        activations.reshape(3072, 1024), out_grads.reshape(3072, 1024),
        proj_in, proj_out, lengths, hess_tiles, train_grads,
    )


def solution(mesh):
    return jax.shard_map(
        on_device,
        mesh=mesh,
        in_specs=(
            P("rows", None, "feat"),
            P("rows", None, "feat"),
            P("feat", None),
            P("feat", None),
            P("rows"),
            P("feat", None, None),
            P("rows", "feat"),
        ),
        out_specs=P("feat", "rows"),
        check_vma=False,
    )
```

```python
import jax
import jax.numpy as jnp
from jax import lax
from jax.experimental import pallas as pl
from jax.experimental.pallas import tpu as pltpu
from jax.sharding import PartitionSpec as P

MESH = pl.DeviceIdType.MESH
BF16 = jnp.bfloat16
F32 = jnp.float32
WAVES = 2
X_ROWS = (512, 768)
FEAT_PEERS = [(dz, dx) for dx in (1, 0) for dz in (2, 1, 3, 0) if (dz, dx) != (0, 0)]
ROW_PEERS = [(1, 0), (0, 2), (0, 1), (0, 3)]
PART_ORDER = [
    ("grad", 2, 0), ("grad", 2, 1), ("act", 2, 1), ("grad", 1, 0), ("grad", 1, 1), ("act", 1, 1),
    ("grad", 3, 0), ("grad", 3, 1), ("act", 3, 1), ("act", 0, 1),
    ("grad", 0, 1), ("act", 2, 0), ("act", 1, 0), ("act", 3, 0), ("grad", 0, 0), ("act", 0, 0),
]


def kernel(
    act, grad, proj_in, proj_out, lengths_hbm, hess, train, out,
    lengths,
    act_v, grad_v, pin_v, pout_v, hess_v, train_v,
    a_send, a_recv, a_own, a_sum, a_recv2,
    g_send, g_recv, g_own, g_sum, g_recv2,
    kron_send, kron_recv, kron_f32, kron_lhs,
    gathered, score_f32, score_send, x_recv, x_sum, x_recv2, z_recv, z_sum, z_recv2,
    load_sem, a_ss, a_rs, g_ss, g_rs, kron_ss, kron_rs,
    row_ss, row_rs, core_ss, core_rs, xs_ss, xs_rs, zs_ss, zs_rs,
):
    r = lax.axis_index("rows")
    f = lax.axis_index("feat")
    xh, y, c = r // 8, (r // 2) % 4, r % 2
    z, xl = f // 2, f % 2

    def feat_at(dz, dx):
        return lax.rem(z + dz, 4) * 2 + lax.rem(xl + dx, 2)

    def rows_at(dx, dy):
        return lax.rem(xh + dx, 2) * 8 + lax.rem(y + dy, 4) * 2 + c

    other_core = (r - c + (1 - c), f)
    sends = []

    def send(src, dst, ssem, rsem, target):
        copy = pltpu.make_async_remote_copy(
            src, dst, ssem, rsem, device_id=target, device_id_type=MESH
        )
        copy.start()
        sends.append(copy)
        return copy

    barrier = pltpu.get_barrier_semaphore()
    targets = [(r, feat_at(*p)) for p in FEAT_PEERS]
    targets += [(rows_at(*p), f) for p in ROW_PEERS] + [other_core]
    for target in targets:
        pl.semaphore_signal(barrier, 1, device_id=target, device_id_type=MESH)

    loads = {}

    def load(key, src, dst, sem):
        loads[key] = pltpu.make_async_copy(src, dst, load_sem.at[sem])
        loads[key].start()

    load("pin", proj_in, pin_v, 0)
    load("pout", proj_out, pout_v, 1)
    load("lengths", lengths_hbm, lengths, 4 + WAVES * 16)
    for w in range(WAVES):
        for k, (which, dz, dx) in enumerate(PART_ORDER):
            row = pl.multiple_of((w * 16 + feat_at(dz, dx) * 2) * 96, 192)
            src, dst = (act, act_v) if which == "act" else (grad, grad_v)
            load(
                (w, which, dz, dx), src.at[pl.ds(row, 192)], dst.at[w, dz * 2 + dx],
                4 + w * 16 + k,
            )

    a_copies, g_copies = {}, {}
    for w in range(WAVES):
        for k, (which, dz, dx) in enumerate(PART_ORDER):
            if w == 0 and k == 0:
                loads["pin"].wait()
                loads["pout"].wait()
            loads[w, which, dz, dx].wait()
            if which == "act":
                part = jnp.dot(act_v[w, dz * 2 + dx], pin_v[...], preferred_element_type=F32)
                if dx == 0:
                    a_own[w, dz] = part
                    continue
                a_send[w, dz] = part.astype(BF16)
            else:
                part = jnp.dot(grad_v[w, dz * 2 + dx], pout_v[...], preferred_element_type=F32)
                if dz == 0:
                    g_own[w, dx] = part
                    continue
                g_send[w, dz - 1, dx] = part.astype(BF16)
                if dx == 0:
                    continue
            if w == 0 and k == 1:
                pl.semaphore_wait(barrier, len(targets))
            if w > 0:
                earlier = (a_copies if which == "act" else g_copies)[w - 1, dz]
                earlier.wait_send()
                sends[:] = [copy for copy in sends if copy is not earlier]
            if which == "act":
                a_copies[w, dz] = send(
                    a_send.at[w, dz], a_recv.at[w, dz], a_ss.at[w, dz], a_rs.at[w, dz],
                    (r, feat_at(0, 1)),
                )
            else:
                g_copies[w, dz] = send(
                    g_send.at[w, dz - 1], g_recv.at[w, dz - 1], g_ss.at[w, dz], g_rs.at[w, dz],
                    (r, feat_at(dz, 0)),
                )
        if w == 0:
            load("hess", hess, hess_v, 2)
    load("train", train, train_v, 3)

    def part_stage(w):
        for dz in (2, 1, 3):
            a_copies[w, dz].wait_recv()
            a_sum[w, dz - 1] = (a_own[w, dz] + a_recv[w, dz].astype(F32)).astype(BF16)
            a_copies[w, 3 + dz] = send(
                a_sum.at[w, dz - 1], a_recv2.at[w, dz - 1],
                a_ss.at[w, 3 + dz], a_rs.at[w, 3 + dz], (r, feat_at(dz, 0)),
            )
        for dz in (2, 1, 3):
            g_copies[w, dz].wait_recv()
        g_sum[w] = (
            g_own[w, 1] + g_recv[w, 0, 1].astype(F32)
            + g_recv[w, 1, 1].astype(F32) + g_recv[w, 2, 1].astype(F32)
        ).astype(BF16)
        g_copies[w, 0] = send(
            g_sum.at[w], g_recv2.at[w], g_ss.at[w, 0], g_rs.at[w, 0], (r, feat_at(0, 1))
        )

    def kron_stage(w):
        a_copies[w, 0].wait_recv()
        for dz in (1, 2, 3):
            a_copies[w, 3 + dz].wait_recv()
        g_copies[w, 0].wait_recv()
        low_a = a_own[w, 0] + a_recv[w, 0].astype(F32)
        low_g = g_own[w, 0] + g_recv2[w].astype(F32)
        for dz in range(3):
            low_a = low_a + a_recv2[w, dz].astype(F32)
            low_g = low_g + g_recv[w, dz, 0].astype(F32)
        if w == 0:
            loads["lengths"].wait()
        token = lax.broadcasted_iota(jnp.int32, (96, 128), 0)
        for q in range(2):
            length = lengths[w * 16 + f * 2 + q]
            a = jnp.where(token < length, low_a[q * 96:(q + 1) * 96], 0.0)
            g = jnp.where(token < length, low_g[q * 96:(q + 1) * 96], 0.0)
            a_hi, g_hi = a.astype(BF16), g.astype(BF16)
            a_lo, g_lo = (a - a_hi.astype(F32)).astype(BF16), (g - g_hi.astype(F32)).astype(BF16)

            def outer(left, right):
                return lax.dot_general(
                    left, right, (((0,), (0,)), ((), ())), preferred_element_type=F32
                )

            kron = outer(g_hi, a_hi) + outer(g_hi, a_lo) + outer(g_lo, a_hi)
            kron = kron * (1.0 / jnp.sqrt(jnp.float32(96)))
            kron_send[w, :, q * 128:(q + 1) * 128] = kron.astype(BF16)
        copies = []
        for k, p in enumerate(FEAT_PEERS):
            target = feat_at(*p)
            copies.append(send(
                kron_send.at[w, pl.ds(pl.multiple_of(target * 16, 16), 16)], kron_recv.at[w, f],
                kron_ss.at[w, k], kron_rs.at[w, k], (r, target),
            ))
        kron_recv[w, f] = kron_send[w, pl.ds(pl.multiple_of(f * 16, 16), 16)]
        return copies

    def precond_stage(w, copies):
        for copy in copies:
            copy.wait_recv()
        if w == 0:
            loads["hess"].wait()
        for s in range(8):
            for q in range(2):
                kron_f32[pl.ds((s * 2 + q) * 16, 16), :] = (
                    kron_recv[w, s, :, q * 128:(q + 1) * 128].astype(F32)
                )
        for i in range(16):
            kron_lhs[:, i * 128:(i + 1) * 128] = (
                kron_f32[pl.ds(i, 16, stride=16), :].astype(BF16)
            )
        for b in range(2):
            gathered[w, r, :, b * 1024:(b + 1) * 1024] = jnp.dot(
                kron_lhs[:, b * 1024:(b + 1) * 1024], hess_v[b], preferred_element_type=F32
            ).astype(BF16)

    def share(w, block, k, target):
        return send(
            gathered.at[w, block], gathered.at[w, block], row_ss.at[w, k], row_rs.at[w, k], target
        )

    def forward(w, k, block):
        return send(
            gathered.at[w, block], gathered.at[w, block], core_ss.at[w, k], core_rs.at[w, k],
            other_core,
        )

    def share_stage(w):
        copies = {"x": share(w, r, 0, (rows_at(1, 0), f))}
        for dy in (2, 1, 3):
            copies[0, dy] = share(w, r, dy, (rows_at(0, dy), f))
        return copies, [forward(w, 0, r)]

    def relay_stage(w, copies, forwards):
        copies["x"].wait_recv()
        for dy in (2, 1, 3):
            copies[1, dy] = share(w, rows_at(1, 0), 3 + dy, (rows_at(0, dy), f))
        forwards.append(forward(w, 4, rows_at(1, 0)))

    def gather_stage(w, copies, forwards):
        for dx in range(2):
            for dy in (1, 3, 2):
                copies[dx, dy].wait_recv()
                forwards.append(forward(w, dx * 4 + dy, rows_at(dx, 4 - dy)))
        for copy in forwards:
            copy.wait_recv()

    def rows_for(target, count=32):
        return pl.ds(pl.multiple_of(target * count, count), count)

    starts, widths = [0] * 4, [X_ROWS[0], X_ROWS[1], 1024 - X_ROWS[0], 1024 - X_ROWS[1]]
    for block, before in ((2, 0), (1, 2), (3, 1)):
        starts[block] = starts[before] + widths[before]
    parts = [pl.ds(0, width) for width in widths]
    xs, zs = {}, {}

    def score_matmul(w, block):
        acc = lax.dot_general(
            gathered[w].reshape(256, 2048),
            train_v[starts[block]:starts[block] + widths[block], :],
            (((1,), (1,)), ((), ())), preferred_element_type=F32,
        )
        score_f32[w, block, :, parts[block]] = acc
        score_send[w, block, :, parts[block]] = acc.astype(BF16)

    def score_stage(w):
        if w == 0:
            loads["train"].wait()
        for s in range(2):
            score_matmul(w, s)
            part = parts[s]
            for dz in (2, 1, 3, 0):
                xs[w, s, dz] = send(
                    score_send.at[w, s, rows_for(feat_at(dz, 1)), part],
                    x_recv.at[w, s, dz, :, part],
                    xs_ss.at[w, s, dz], xs_rs.at[w, s, dz], (r, feat_at(0, 1)),
                )
            score_matmul(w, 2 + s)
            part = parts[2 + s]
            for dz in (2, 1, 3):
                zs[w, s, dz] = send(
                    score_send.at[w, 2 + s, rows_for(lax.rem(z + dz, 4), 64), part],
                    z_recv.at[w, s, dz - 1, :, part],
                    zs_ss.at[w, s, dz], zs_rs.at[w, s, dz], (r, feat_at(dz, 0)),
                )

    def score_stage2(w, s):
        part = parts[s]
        for dz in (2, 1, 3):
            xs[w, s, dz].wait_recv()
            x_sum[w, s, dz - 1, :, part] = (
                score_f32[w, s, rows_for(feat_at(dz, 0)), part]
                + x_recv[w, s, dz, :, part].astype(F32)
            ).astype(BF16)
            xs[w, s, 3 + dz] = send(
                x_sum.at[w, s, dz - 1, :, part], x_recv2.at[w, s, dz - 1, :, part],
                xs_ss.at[w, s, 3 + dz], xs_rs.at[w, s, 3 + dz], (r, feat_at(dz, 0)),
            )
        part = parts[2 + s]
        for dz in (2, 1, 3):
            zs[w, s, dz].wait_recv()
        total = score_f32[w, 2 + s, rows_for(feat_at(0, 1)), part]
        for dz in range(3):
            total = total + z_recv[w, s, dz, rows_for(1 - xl), part].astype(F32)
        z_sum[w, s, :, part] = total.astype(BF16)
        zs[w, s, 0] = send(
            z_sum.at[w, s, :, part], z_recv2.at[w, s, :, part],
            zs_ss.at[w, s, 0], zs_rs.at[w, s, 0], (r, feat_at(0, 1)),
        )

    def final_stage(w, s):
        xs[w, s, 0].wait_recv()
        for dz in (1, 2, 3):
            xs[w, s, 3 + dz].wait_recv()
        zs[w, s, 0].wait_recv()
        part, part2 = parts[s], parts[2 + s]
        first = score_f32[w, s, rows_for(f), part] + x_recv[w, s, 0, :, part].astype(F32)
        second = score_f32[w, 2 + s, rows_for(f), part2] + z_recv2[w, s, :, part2].astype(F32)
        for dz in range(3):
            first = first + x_recv2[w, s, dz, :, part].astype(F32)
            second = second + z_recv[w, s, dz, rows_for(xl), part2].astype(F32)
        for core in range(2):
            rows = pl.ds(core * 32 + w * 16, 16)
            half = slice(core * 16, (core + 1) * 16)
            out[rows, pl.ds(starts[s], widths[s])] = first[half] * (1.0 / 128)
            out[rows, pl.ds(starts[2 + s], widths[2 + s])] = second[half] * (1.0 / 128)

    part_stage(0)
    k0 = kron_stage(0)
    part_stage(1)
    precond_stage(0, k0)
    g0 = share_stage(0)
    k1 = kron_stage(1)
    precond_stage(1, k1)
    relay_stage(0, *g0)
    g1 = share_stage(1)
    relay_stage(1, *g1)
    gather_stage(0, *g0)
    score_stage(0)
    gather_stage(1, *g1)
    score_stage(1)
    for w in range(WAVES):
        for s in range(2):
            score_stage2(w, s)
    for w in range(WAVES):
        for s in range(2):
            final_stage(w, s)
    for copy in sends:
        copy.wait_send()


def on_device(activations, out_grads, proj_in, proj_out, lengths, hess_tiles, train_grads):
    hbm = pl.BlockSpec(memory_space=pl.ANY)
    n_feat = len(FEAT_PEERS)
    dma = pltpu.SemaphoreType.DMA
    return pl.pallas_call(
        kernel,
        out_shape=jax.ShapeDtypeStruct((64, 2048), F32),
        in_specs=[hbm, hbm, hbm, hbm, hbm, hbm, hbm],
        out_specs=pl.BlockSpec(memory_space=pltpu.VMEM),
        scratch_shapes=[
            pltpu.SMEM((32,), jnp.int32),
            pltpu.VMEM((WAVES, 8, 192, 1024), BF16),
            pltpu.VMEM((WAVES, 8, 192, 1024), BF16),
            pltpu.VMEM((1024, 128), BF16),
            pltpu.VMEM((1024, 128), BF16),
            pltpu.VMEM((2, 1024, 1024), BF16),
            pltpu.VMEM((2048, 2048), BF16),
            pltpu.VMEM((WAVES, 4, 192, 128), BF16),
            pltpu.VMEM((WAVES, 4, 192, 128), BF16),
            pltpu.VMEM((WAVES, 4, 192, 128), F32),
            pltpu.VMEM((WAVES, 3, 192, 128), BF16),
            pltpu.VMEM((WAVES, 3, 192, 128), BF16),
            pltpu.VMEM((WAVES, 3, 2, 192, 128), BF16),
            pltpu.VMEM((WAVES, 3, 2, 192, 128), BF16),
            pltpu.VMEM((WAVES, 2, 192, 128), F32),
            pltpu.VMEM((WAVES, 192, 128), BF16),
            pltpu.VMEM((WAVES, 192, 128), BF16),
            pltpu.VMEM((WAVES, 128, 256), BF16),
            pltpu.VMEM((WAVES, 8, 16, 256), BF16),
            pltpu.VMEM((256, 128), F32),
            pltpu.VMEM((16, 2048), BF16),
            pltpu.VMEM((WAVES, 16, 16, 2048), BF16),
            pltpu.VMEM((WAVES, 4, 256, 768), F32),
            pltpu.VMEM((WAVES, 4, 256, 768), BF16),
            pltpu.VMEM((WAVES, 2, 4, 32, 768), BF16),
            pltpu.VMEM((WAVES, 2, 3, 32, 768), BF16),
            pltpu.VMEM((WAVES, 2, 3, 32, 768), BF16),
            pltpu.VMEM((WAVES, 2, 3, 64, 768), BF16),
            pltpu.VMEM((WAVES, 2, 32, 768), BF16),
            pltpu.VMEM((WAVES, 2, 32, 768), BF16),
            dma((5 + WAVES * 16,)),
            dma((WAVES, 7)), dma((WAVES, 7)),
            dma((WAVES, 4)), dma((WAVES, 4)),
            dma((WAVES, n_feat)), dma((WAVES, n_feat)),
            dma((WAVES, 7)), dma((WAVES, 7)),
            dma((WAVES, 8)), dma((WAVES, 8)),
            dma((WAVES, 2, 7)), dma((WAVES, 2, 7)),
            dma((WAVES, 2, 4)), dma((WAVES, 2, 4)),
        ],
        compiler_params=pltpu.CompilerParams(
            collective_id=0, has_side_effects=True, vmem_limit_bytes=56 * 1024 * 1024
        ),
        cost_estimate=pl.CostEstimate(
            flops=6_000_000_000, bytes_accessed=26_000_000, transcendentals=0
        ),
        name="influence",
    )(
        activations.reshape(3072, 1024), out_grads.reshape(3072, 1024),
        proj_in, proj_out, lengths, hess_tiles, train_grads,
    )


def solution(mesh):
    return jax.shard_map(
        on_device,
        mesh=mesh,
        in_specs=(
            P("rows", None, "feat"),
            P("rows", None, "feat"),
            P("feat", None),
            P("feat", None),
            P("rows"),
            P("feat", None, None),
            P("rows", "feat"),
        ),
        out_specs=P("feat", "rows"),
        check_vma=False,
    )
```

```python
import jax
import jax.numpy as jnp
from jax import lax
from jax.experimental import pallas as pl
from jax.experimental.pallas import tpu as pltpu
from jax.sharding import PartitionSpec as P

MESH = pl.DeviceIdType.MESH
BF16 = jnp.bfloat16
F32 = jnp.float32
WAVES = 2
X_ROWS = (512, 768)
FEAT_PEERS = [(dz, dx) for dx in (1, 0) for dz in (2, 1, 3, 0) if (dz, dx) != (0, 0)]
ROW_PEERS = [(1, 0), (0, 2), (0, 1), (0, 3)]
PART_ORDER = [
    ("grad", 2, 0), ("grad", 2, 1), ("act", 2, 1), ("grad", 1, 0), ("grad", 1, 1), ("act", 1, 1),
    ("grad", 3, 0), ("grad", 3, 1), ("act", 3, 1), ("act", 0, 1),
    ("grad", 0, 1), ("act", 2, 0), ("act", 1, 0), ("act", 3, 0), ("grad", 0, 0), ("act", 0, 0),
]


def kernel(
    act, grad, proj_in, proj_out, lengths_hbm, hess, train, out,
    lengths,
    act_v, grad_v, pin_v, pout_v, hess_v, train_v,
    a_send, a_recv, a_own, a_sum, a_recv2,
    g_send, g_recv, g_own, g_sum, g_recv2,
    kron_send, kron_recv, kron_f32, kron_lhs,
    gathered, score_f32, score_send, x_recv, x_sum, x_recv2, z_recv, z_sum, z_recv2,
    load_sem, a_ss, a_rs, g_ss, g_rs, kron_ss, kron_rs,
    row_ss, row_rs, core_ss, core_rs, xs_ss, xs_rs, zs_ss, zs_rs,
):
    r = lax.axis_index("rows")
    f = lax.axis_index("feat")
    xh, y, c = r // 8, (r // 2) % 4, r % 2
    z, xl = f // 2, f % 2

    def feat_at(dz, dx):
        return lax.rem(z + dz, 4) * 2 + lax.rem(xl + dx, 2)

    def rows_at(dx, dy):
        return lax.rem(xh + dx, 2) * 8 + lax.rem(y + dy, 4) * 2 + c

    other_core = (r - c + (1 - c), f)
    sends = []

    def send(src, dst, ssem, rsem, target):
        copy = pltpu.make_async_remote_copy(
            src, dst, ssem, rsem, device_id=target, device_id_type=MESH
        )
        copy.start()
        sends.append(copy)
        return copy

    barrier = pltpu.get_barrier_semaphore()
    targets = [(r, feat_at(*p)) for p in FEAT_PEERS]
    targets += [(rows_at(*p), f) for p in ROW_PEERS] + [other_core]
    for target in targets:
        pl.semaphore_signal(barrier, 1, device_id=target, device_id_type=MESH)

    loads = {}

    def load(key, src, dst, sem):
        loads[key] = pltpu.make_async_copy(src, dst, load_sem.at[sem])
        loads[key].start()

    load("pin", proj_in, pin_v, 0)
    load("pout", proj_out, pout_v, 1)
    load("lengths", lengths_hbm, lengths, 4 + WAVES * 16)
    for w in range(WAVES):
        for k, (which, dz, dx) in enumerate(PART_ORDER):
            row = pl.multiple_of((w * 16 + feat_at(dz, dx) * 2) * 96, 192)
            src, dst = (act, act_v) if which == "act" else (grad, grad_v)
            load(
                (w, which, dz, dx), src.at[pl.ds(row, 192)], dst.at[w, dz * 2 + dx],
                4 + w * 16 + k,
            )

    a_copies, g_copies = {}, {}
    for w in range(WAVES):
        for k, (which, dz, dx) in enumerate(PART_ORDER):
            if w == 0 and k == 0:
                loads["pin"].wait()
                loads["pout"].wait()
            loads[w, which, dz, dx].wait()
            if which == "act":
                part = jnp.dot(act_v[w, dz * 2 + dx], pin_v[...], preferred_element_type=F32)
                if dx == 0:
                    a_own[w, dz] = part
                    continue
                a_send[w, dz] = part.astype(BF16)
            else:
                part = jnp.dot(grad_v[w, dz * 2 + dx], pout_v[...], preferred_element_type=F32)
                if dz == 0:
                    g_own[w, dx] = part
                    continue
                g_send[w, dz - 1, dx] = part.astype(BF16)
                if dx == 0:
                    continue
            if w == 0 and k == 1:
                pl.semaphore_wait(barrier, len(targets))
            if w > 0:
                earlier = (a_copies if which == "act" else g_copies)[w - 1, dz]
                earlier.wait_send()
                sends[:] = [copy for copy in sends if copy is not earlier]
            if which == "act":
                a_copies[w, dz] = send(
                    a_send.at[w, dz], a_recv.at[w, dz], a_ss.at[w, dz], a_rs.at[w, dz],
                    (r, feat_at(0, 1)),
                )
            else:
                g_copies[w, dz] = send(
                    g_send.at[w, dz - 1], g_recv.at[w, dz - 1], g_ss.at[w, dz], g_rs.at[w, dz],
                    (r, feat_at(dz, 0)),
                )
        if w == 0:
            load("hess", hess, hess_v, 2)
    load("train", train, train_v, 3)

    def part_stage(w):
        for dz in (2, 1, 3):
            a_copies[w, dz].wait_recv()
            a_sum[w, dz - 1] = (a_own[w, dz] + a_recv[w, dz].astype(F32)).astype(BF16)
            a_copies[w, 3 + dz] = send(
                a_sum.at[w, dz - 1], a_recv2.at[w, dz - 1],
                a_ss.at[w, 3 + dz], a_rs.at[w, 3 + dz], (r, feat_at(dz, 0)),
            )
        for dz in (2, 1, 3):
            g_copies[w, dz].wait_recv()
        g_sum[w] = (
            g_own[w, 1] + g_recv[w, 0, 1].astype(F32)
            + g_recv[w, 1, 1].astype(F32) + g_recv[w, 2, 1].astype(F32)
        ).astype(BF16)
        g_copies[w, 0] = send(
            g_sum.at[w], g_recv2.at[w], g_ss.at[w, 0], g_rs.at[w, 0], (r, feat_at(0, 1))
        )

    def kron_stage(w):
        a_copies[w, 0].wait_recv()
        for dz in (1, 2, 3):
            a_copies[w, 3 + dz].wait_recv()
        g_copies[w, 0].wait_recv()
        low_a = a_own[w, 0] + a_recv[w, 0].astype(F32)
        low_g = g_own[w, 0] + g_recv2[w].astype(F32)
        for dz in range(3):
            low_a = low_a + a_recv2[w, dz].astype(F32)
            low_g = low_g + g_recv[w, dz, 0].astype(F32)
        if w == 0:
            loads["lengths"].wait()
        token = lax.broadcasted_iota(jnp.int32, (96, 128), 0)
        for q in range(2):
            length = lengths[w * 16 + f * 2 + q]
            a = jnp.where(token < length, low_a[q * 96:(q + 1) * 96], 0.0)
            g = jnp.where(token < length, low_g[q * 96:(q + 1) * 96], 0.0)
            a_hi, g_hi = a.astype(BF16), g.astype(BF16)
            a_lo, g_lo = (a - a_hi.astype(F32)).astype(BF16), (g - g_hi.astype(F32)).astype(BF16)

            def outer(left, right):
                return lax.dot_general(
                    left, right, (((0,), (0,)), ((), ())), preferred_element_type=F32
                )

            kron = outer(g_hi, a_hi) + outer(g_hi, a_lo) + outer(g_lo, a_hi)
            kron = kron * (1.0 / jnp.sqrt(jnp.float32(96)))
            kron_send[w, :, q * 128:(q + 1) * 128] = kron.astype(BF16)
        copies = []
        for k, p in enumerate(FEAT_PEERS):
            target = feat_at(*p)
            copies.append(send(
                kron_send.at[w, pl.ds(pl.multiple_of(target * 16, 16), 16)], kron_recv.at[w, f],
                kron_ss.at[w, k], kron_rs.at[w, k], (r, target),
            ))
        kron_recv[w, f] = kron_send[w, pl.ds(pl.multiple_of(f * 16, 16), 16)]
        return copies

    def precond_stage(w, copies):
        for copy in copies:
            copy.wait_recv()
        if w == 0:
            loads["hess"].wait()
        for s in range(8):
            for q in range(2):
                kron_f32[pl.ds((s * 2 + q) * 16, 16), :] = (
                    kron_recv[w, s, :, q * 128:(q + 1) * 128].astype(F32)
                )
        for i in range(16):
            kron_lhs[:, i * 128:(i + 1) * 128] = (
                kron_f32[pl.ds(i, 16, stride=16), :].astype(BF16)
            )
        for b in range(2):
            gathered[w, r, :, b * 1024:(b + 1) * 1024] = jnp.dot(
                kron_lhs[:, b * 1024:(b + 1) * 1024], hess_v[b], preferred_element_type=F32
            ).astype(BF16)

    def share(w, block, k, target):
        return send(
            gathered.at[w, block], gathered.at[w, block], row_ss.at[w, k], row_rs.at[w, k], target
        )

    def forward(w, k, block):
        return send(
            gathered.at[w, block], gathered.at[w, block], core_ss.at[w, k], core_rs.at[w, k],
            other_core,
        )

    def share_stage(w):
        copies = {"x": share(w, r, 0, (rows_at(1, 0), f))}
        for dy in (2, 1, 3):
            copies[0, dy] = share(w, r, dy, (rows_at(0, dy), f))
        return copies, [forward(w, 0, r)]

    def relay_stage(w, copies, forwards):
        copies["x"].wait_recv()
        for dy in (2, 1, 3):
            copies[1, dy] = share(w, rows_at(1, 0), 3 + dy, (rows_at(0, dy), f))
        forwards.append(forward(w, 4, rows_at(1, 0)))

    def gather_stage(w, copies, forwards):
        for dx in range(2):
            for dy in (1, 3, 2):
                copies[dx, dy].wait_recv()
                forwards.append(forward(w, dx * 4 + dy, rows_at(dx, 4 - dy)))
        for copy in forwards:
            copy.wait_recv()

    def rows_for(target, count=32):
        return pl.ds(pl.multiple_of(target * count, count), count)

    starts, widths = [0] * 4, [X_ROWS[0], X_ROWS[1], 1024 - X_ROWS[0], 1024 - X_ROWS[1]]
    for block, before in ((2, 0), (1, 2), (3, 1)):
        starts[block] = starts[before] + widths[before]
    parts = [pl.ds(0, width) for width in widths]
    xs, zs = {}, {}

    def score_matmul(w, block):
        acc = lax.dot_general(
            gathered[w].reshape(256, 2048),
            train_v[starts[block]:starts[block] + widths[block], :],
            (((1,), (1,)), ((), ())), preferred_element_type=F32,
        )
        score_f32[w, block, :, parts[block]] = acc
        score_send[w, block, :, parts[block]] = acc.astype(BF16)

    def score_stage(w):
        if w == 0:
            loads["train"].wait()
        for s in range(2):
            score_matmul(w, s)
            part = parts[s]
            for dz in (2, 1, 3, 0):
                xs[w, s, dz] = send(
                    score_send.at[w, s, rows_for(feat_at(dz, 1)), part],
                    x_recv.at[w, s, dz, :, part],
                    xs_ss.at[w, s, dz], xs_rs.at[w, s, dz], (r, feat_at(0, 1)),
                )
            score_matmul(w, 2 + s)
            part = parts[2 + s]
            for dz in (2, 1, 3):
                zs[w, s, dz] = send(
                    score_send.at[w, 2 + s, rows_for(lax.rem(z + dz, 4), 64), part],
                    z_recv.at[w, s, dz - 1, :, part],
                    zs_ss.at[w, s, dz], zs_rs.at[w, s, dz], (r, feat_at(dz, 0)),
                )

    def score_stage2(w, s):
        part = parts[s]
        for dz in (2, 1, 3):
            xs[w, s, dz].wait_recv()
            x_sum[w, s, dz - 1, :, part] = (
                score_f32[w, s, rows_for(feat_at(dz, 0)), part]
                + x_recv[w, s, dz, :, part].astype(F32)
            ).astype(BF16)
            xs[w, s, 3 + dz] = send(
                x_sum.at[w, s, dz - 1, :, part], x_recv2.at[w, s, dz - 1, :, part],
                xs_ss.at[w, s, 3 + dz], xs_rs.at[w, s, 3 + dz], (r, feat_at(dz, 0)),
            )
        part = parts[2 + s]
        for dz in (2, 1, 3):
            zs[w, s, dz].wait_recv()
        total = score_f32[w, 2 + s, rows_for(feat_at(0, 1)), part]
        for dz in range(3):
            total = total + z_recv[w, s, dz, rows_for(1 - xl), part].astype(F32)
        z_sum[w, s, :, part] = total.astype(BF16)
        zs[w, s, 0] = send(
            z_sum.at[w, s, :, part], z_recv2.at[w, s, :, part],
            zs_ss.at[w, s, 0], zs_rs.at[w, s, 0], (r, feat_at(0, 1)),
        )

    def final_stage(w, s):
        xs[w, s, 0].wait_recv()
        for dz in (1, 2, 3):
            xs[w, s, 3 + dz].wait_recv()
        zs[w, s, 0].wait_recv()
        part, part2 = parts[s], parts[2 + s]
        first = score_f32[w, s, rows_for(f), part] + x_recv[w, s, 0, :, part].astype(F32)
        second = score_f32[w, 2 + s, rows_for(f), part2] + z_recv2[w, s, :, part2].astype(F32)
        for dz in range(3):
            first = first + x_recv2[w, s, dz, :, part].astype(F32)
            second = second + z_recv[w, s, dz, rows_for(xl), part2].astype(F32)
        for core in range(2):
            rows = pl.ds(core * 32 + w * 16, 16)
            half = slice(core * 16, (core + 1) * 16)
            out[rows, pl.ds(starts[s], widths[s])] = first[half] * (1.0 / 128)
            out[rows, pl.ds(starts[2 + s], widths[2 + s])] = second[half] * (1.0 / 128)

    part_stage(0)
    k0 = kron_stage(0)
    part_stage(1)
    precond_stage(0, k0)
    g0 = share_stage(0)
    k1 = kron_stage(1)
    precond_stage(1, k1)
    relay_stage(0, *g0)
    g1 = share_stage(1)
    relay_stage(1, *g1)
    gather_stage(0, *g0)
    score_stage(0)
    gather_stage(1, *g1)
    score_stage(1)
    for w in range(WAVES):
        for s in range(2):
            score_stage2(w, s)
    for w in range(WAVES):
        for s in range(2):
            final_stage(w, s)
    for copy in sends:
        copy.wait_send()


def on_device(activations, out_grads, proj_in, proj_out, lengths, hess_tiles, train_grads):
    hbm = pl.BlockSpec(memory_space=pl.ANY)
    n_feat = len(FEAT_PEERS)
    dma = pltpu.SemaphoreType.DMA
    return pl.pallas_call(
        kernel,
        out_shape=jax.ShapeDtypeStruct((64, 2048), F32),
        in_specs=[hbm, hbm, hbm, hbm, hbm, hbm, hbm],
        out_specs=pl.BlockSpec(memory_space=pltpu.VMEM),
        scratch_shapes=[
            pltpu.SMEM((32,), jnp.int32),
            pltpu.VMEM((WAVES, 8, 192, 1024), BF16),
            pltpu.VMEM((WAVES, 8, 192, 1024), BF16),
            pltpu.VMEM((1024, 128), BF16),
            pltpu.VMEM((1024, 128), BF16),
            pltpu.VMEM((2, 1024, 1024), BF16),
            pltpu.VMEM((2048, 2048), BF16),
            pltpu.VMEM((WAVES, 4, 192, 128), BF16),
            pltpu.VMEM((WAVES, 4, 192, 128), BF16),
            pltpu.VMEM((WAVES, 4, 192, 128), F32),
            pltpu.VMEM((WAVES, 3, 192, 128), BF16),
            pltpu.VMEM((WAVES, 3, 192, 128), BF16),
            pltpu.VMEM((WAVES, 3, 2, 192, 128), BF16),
            pltpu.VMEM((WAVES, 3, 2, 192, 128), BF16),
            pltpu.VMEM((WAVES, 2, 192, 128), F32),
            pltpu.VMEM((WAVES, 192, 128), BF16),
            pltpu.VMEM((WAVES, 192, 128), BF16),
            pltpu.VMEM((WAVES, 128, 256), BF16),
            pltpu.VMEM((WAVES, 8, 16, 256), BF16),
            pltpu.VMEM((272, 128), F32),
            pltpu.VMEM((16, 2048), BF16),
            pltpu.VMEM((WAVES, 16, 16, 2048), BF16),
            pltpu.VMEM((WAVES, 4, 256, 768), F32),
            pltpu.VMEM((WAVES, 4, 256, 768), BF16),
            pltpu.VMEM((WAVES, 2, 4, 32, 768), BF16),
            pltpu.VMEM((WAVES, 2, 3, 32, 768), BF16),
            pltpu.VMEM((WAVES, 2, 3, 32, 768), BF16),
            pltpu.VMEM((WAVES, 2, 3, 64, 768), BF16),
            pltpu.VMEM((WAVES, 2, 32, 768), BF16),
            pltpu.VMEM((WAVES, 2, 32, 768), BF16),
            dma((5 + WAVES * 16,)),
            dma((WAVES, 7)), dma((WAVES, 7)),
            dma((WAVES, 4)), dma((WAVES, 4)),
            dma((WAVES, n_feat)), dma((WAVES, n_feat)),
            dma((WAVES, 7)), dma((WAVES, 7)),
            dma((WAVES, 8)), dma((WAVES, 8)),
            dma((WAVES, 2, 7)), dma((WAVES, 2, 7)),
            dma((WAVES, 2, 4)), dma((WAVES, 2, 4)),
        ],
        compiler_params=pltpu.CompilerParams(
            collective_id=0, has_side_effects=True, vmem_limit_bytes=56 * 1024 * 1024
        ),
        cost_estimate=pl.CostEstimate(
            flops=6_000_000_000, bytes_accessed=26_000_000, transcendentals=0
        ),
        name="influence",
    )(
        activations.reshape(3072, 1024), out_grads.reshape(3072, 1024),
        proj_in, proj_out, lengths, hess_tiles, train_grads,
    )


def solution(mesh):
    return jax.shard_map(
        on_device,
        mesh=mesh,
        in_specs=(
            P("rows", None, "feat"),
            P("rows", None, "feat"),
            P("feat", None),
            P("feat", None),
            P("rows"),
            P("feat", None, None),
            P("rows", "feat"),
        ),
        out_specs=P("feat", "rows"),
        check_vma=False,
    )
```
